32 devices in a mesh: groups: 2 (over x), tensor: 16 (over z, y, core).
Axes of the slice: x: 2, y: 2, z: 4, core: 2. Of those that a mesh axis runs over, the one named last changes fastest.
Arguments:
- mixer_in: bfloat16 [1024, 4096], P('groups', 'tensor'), parts along dimension 0, may hold values from -6 to 6
- gate_in: bfloat16 [1024, 4096], P('groups', 'tensor'), parts along dimension 0, may hold values from -6 to 6
- conv_tail: bfloat16 [3, 256, 4096], P(None, 'groups', 'tensor'), parts along dimension 1, may hold values from -6 to 6
- ssm_state: bfloat16 [256, 16, 4096], P('groups', None, 'tensor'), parts along dimension 0, may hold values from -6 to 6
- resid: bfloat16 [1024, 8192], P(('groups', 'tensor')), parts along dimension 0, may hold values from -6 to 6
- expert_ids: int32 [1024, 2], P('groups'), parts along dimension 0, may hold values from 0 to 15, as said below
- conv_weight: bfloat16 [4, 4096], P(None, 'tensor'), may hold values from -3 to 3
- conv_bias: float32 [4096], P('tensor'), may hold values from -3 to 3
- x_weight: bfloat16 [4096, 544], P('tensor'), may hold values from -0.09375 to 0.09375
- dt_weight: bfloat16 [512, 4096], P(None, 'tensor'), may hold values from -0.25 to 0.25
- dt_bias: float32 [4096], P('tensor'), may hold values from -4 to -1
- decay_log: float32 [16, 4096], P(None, 'tensor'), may hold values from -1 to 2.5
- skip_gain: float32 [4096], P('tensor'), may hold values from 0.5 to 1.5
- out_weight: bfloat16 [4096, 8192], P('tensor'), may hold values from -0.09375 to 0.09375
- norm_gain: bfloat16 [8192], replicated, may hold values from 0.5 to 2
- router_weight: bfloat16 [8192, 16], replicated, may hold values from -0.0625 to 0.0625
- w_gate: bfloat16 [8192, 6144], P(None, 'tensor'), may hold values from -0.0625 to 0.0625
- w_up: bfloat16 [8192, 6144], P(None, 'tensor'), may hold values from -0.0625 to 0.0625
- w_down: bfloat16 [6144, 8192], P('tensor'), may hold values from -0.078125 to 0.078125
Outputs:
- layer_out: bfloat16 [1024, 8192], P(('groups', 'tensor')), parts along dimension 0
- state_out: bfloat16 [256, 16, 4096], P('groups', None, 'tensor'), parts along dimension 0
The draws below stay inside these ranges and needn't reach their ends.
There are 2 independent parts, one for each index of `groups`. The reference program is written for one: setup_inputs(seed, part) draws one part's arguments, and reference() takes and returns one part's arrays. A program takes and returns all parts, laid end to end along the dimension named above; an argument that names none is the same for every part. Nothing has to cross between parts.
Inputs may be any that keep to these rules, and one draw needn't show every extreme that they name: `expert_ids`: the two ids of a token differ. In each aligned block of 32 tokens at least one and at most 12 tokens name expert 0, and in some block exactly 12 do.
All inputs are finite; a program needn't handle non-finite values.
Results may differ from the reference program's by a relative error of at most 0.023.
Values may be sent and summed in bfloat16 or wider, within the bound.
A program may use at most 192 MiB of HBM per device.

```python
import math
import jax
import jax.numpy as jnp
from jax import lax

D = 8192
RANK = 512
STATE = 16
CONV = 4
EXPERTS = 16
E_DEV = 256
FF_DEV = 384
STEPS = 4
REQ = 128
TOKENS = 512
ROWS = 32
MOST = 12
FF_WIN = 6144
E = 4096
PROJ = 544
N_TENSOR = 16


def draw_expert_ids(key, part):
    key = jax.random.fold_in(key, 11)
    keys = jax.random.split(key, 6)
    blocks = TOKENS // ROWS
    counts = jax.random.randint(keys[0], (blocks,), 1, MOST + 1)
    forced = jax.random.randint(keys[1], (), 0, blocks)
    counts = jnp.where(jnp.arange(blocks) == forced, MOST, counts)
    ranks = jax.vmap(lambda k: jax.random.permutation(k, ROWS))(jax.random.split(keys[2], blocks))
    hits = ranks < counts[:, None]
    other = jax.random.randint(keys[3], (blocks, ROWS), 1, EXPERTS)
    step = jax.random.randint(keys[4], (blocks, ROWS), 1, EXPERTS - 1)
    second = 1 + (other - 1 + step) % (EXPERTS - 1)
    flip = jax.random.randint(keys[5], (blocks, ROWS), 0, 2) > 0
    zero = jnp.zeros_like(other)
    first_id = jnp.where(hits, jnp.where(flip, other, zero), other)
    second_id = jnp.where(hits, jnp.where(flip, zero, other), second)
    return jnp.stack([first_id, second_id], axis=-1).reshape(TOKENS, 2).astype(jnp.int32)


def steps_of(stream_key, extent, pieces, low, top_value):
    def one(dim, blocks):
        heights = jax.random.uniform(jax.random.fold_in(jax.random.fold_in(stream_key, 6), dim), (blocks,), jnp.float32, low / len(pieces), top_value / len(pieces))
        return jnp.repeat(jnp.exp(heights), extent[dim] // blocks).reshape((-1,) + (1,) * (len(extent) - dim - 1))

    gain = one(*pieces[0])
    for cut in pieces[1:]:
        gain = gain * one(*cut)
    return gain


def centred(key, extent, scale, reach, cuts=(), held_as=jnp.bfloat16):
    result = jax.random.normal(key, extent, jnp.float32) * scale
    if len(cuts) > 0:
        result = steps_of(key, extent, cuts, -0.22, 0.18) * result
    return jnp.clip(result, min=-reach, max=reach).astype(held_as)


def setup_inputs(seed: int = 0, part: int = 0) -> dict:
    splits = jax.random.split(jax.random.key(seed), 20)
    part_splits = jax.random.split(jax.random.fold_in(splits[19], part), 20)
    return {
        "mixer_in": centred(part_splits[0], (TOKENS, E), 1.0, 6.0, ((1, 16),)),
        "gate_in": centred(part_splits[1], (TOKENS, E), 1.0, 6.0, ((1, 16),)),
        "conv_tail": centred(part_splits[2], (CONV - 1, REQ, E), 1.0, 6.0, ((2, 16),)),
        "ssm_state": centred(part_splits[3], (REQ, STATE, E), 1.0, 6.0, ((2, 16),)),
        "resid": centred(part_splits[4], (TOKENS, D), 1.0, 6.0, ((0, 16),)),
        "expert_ids": draw_expert_ids(jax.random.fold_in(jax.random.fold_in(splits[19], part), 71), part),
        "conv_weight": centred(splits[6], (CONV, E), CONV ** -0.5, 3.0, ((1, 16),)),
        "conv_bias": centred(splits[7], (E,), 0.5, 3.0, ((0, 16),), jnp.float32),
        "x_weight": centred(splits[8], (E, PROJ), E ** -0.5, 0.09375, ((0, 16),)),
        "dt_weight": centred(splits[9], (RANK, E), RANK ** -0.5, 0.25, ((1, 16),)),
        "dt_bias": jnp.clip(-4.0 + 3.0 * jax.random.uniform(splits[10], (E,), jnp.float32) ** steps_of(splits[10], (E,), ((0, 16),), -0.2, 0.2), -4.0, -1.0),
        "decay_log": jnp.clip(-1.0 + 3.5 * jax.random.uniform(splits[11], (STATE, E), jnp.float32) ** steps_of(splits[11], (STATE, E), ((1, 16),), -0.2, 0.2), -1.0, 2.5),
        "skip_gain": jnp.clip(0.5 + 1.0 * jax.random.uniform(splits[12], (E,), jnp.float32) ** steps_of(splits[12], (E,), ((0, 16),), -0.2, 0.2), 0.5, 1.5),
        "out_weight": centred(splits[13], (E, D), E ** -0.5, 0.09375, ((0, 16),)),
        "norm_gain": jnp.clip(jnp.exp(jax.random.uniform(splits[14], (D,), jnp.float32, math.log(0.5), math.log(2.0))), 0.5, 2.0).astype(jnp.bfloat16),
        "router_weight": centred(splits[15], (D, EXPERTS), D ** -0.5, 0.0625),
        "w_gate": centred(splits[16], (D, FF_WIN), D ** -0.5, 0.0625, ((1, 16),)),
        "w_up": centred(splits[17], (D, FF_WIN), D ** -0.5, 0.0625, ((1, 16),)),
        "w_down": centred(splits[18], (FF_WIN, D), FF_WIN ** -0.5, 0.078125, ((0, 16),)),
    }


EPSILON = 1e-06

def convolve(mixer_in, conv_tail, conv_weight, conv_bias):
    width = mixer_in.shape[1]
    inputs = mixer_in.reshape(STEPS, REQ, width).astype(jnp.float32)
    history = jnp.concatenate([conv_tail.astype(jnp.float32), inputs], axis=0)
    kernel = conv_weight.astype(jnp.float32)
    summed = conv_bias[None, None, :] + kernel[0] * history[0:STEPS]
    for offset in range(1, CONV):
        summed = summed + kernel[offset] * history[offset:offset + STEPS]
    return jax.nn.silu(summed).astype(jnp.bfloat16).reshape(STEPS * REQ, width)

def run_states(mixed, gate_in, delta, b_part, c_part, ssm_state, decay_log, skip_gain):
    rate = -jnp.exp(decay_log)
    state = ssm_state.astype(jnp.float32)
    results = []
    for position in range(STEPS):
        first = position * REQ
        step_delta = delta[first:first + REQ]
        step_input = mixed[first:first + REQ].astype(jnp.float32)
        decay = jnp.exp(step_delta[:, None, :] * rate[None, :, :])
        state = decay * state + (step_delta * step_input)[:, None, :] * b_part[first:first + REQ][:, :, None]
        reading = lax.optimization_barrier(jnp.sum(c_part[first:first + REQ][:, :, None] * state, axis=1)) + skip_gain[None, :] * step_input
        results.append(reading * jax.nn.silu(gate_in[first:first + REQ].astype(jnp.float32)))
    return (jnp.concatenate(results, axis=0).astype(jnp.bfloat16), state.astype(jnp.bfloat16))

def route_inputs(hidden_state, expert_ids, norm_gain, router_weight):
    scale = lax.rsqrt(lax.optimization_barrier(jnp.mean(hidden_state * hidden_state, axis=1, keepdims=True)) + EPSILON)
    normed = (hidden_state * scale * norm_gain.astype(jnp.float32)[None, :]).astype(jnp.bfloat16)
    logits = jnp.dot(normed, router_weight, preferred_element_type=jnp.float32)
    labels = jnp.arange(logits.shape[1], dtype=jnp.int32)
    onehot = expert_ids[:, :, None] == labels[None, None, :]
    picked = lax.optimization_barrier(jnp.sum(jnp.where(onehot, logits[:, None, :], 0.0), axis=2))
    weight_first = jax.nn.sigmoid(picked[:, 0] - picked[:, 1])
    weight_second = jax.nn.sigmoid(picked[:, 1] - picked[:, 0])
    route_weight = jnp.where(expert_ids[:, 0] == 0, weight_first, jnp.where(expert_ids[:, 1] == 0, weight_second, 0.0))
    return (normed, route_weight)

def reference(mixer_in, gate_in, conv_tail, ssm_state, resid, expert_ids, conv_weight, conv_bias, x_weight, dt_weight, dt_bias, decay_log, skip_gain, out_weight, norm_gain, router_weight, w_gate, w_up, w_down):
    mixed = convolve(mixer_in, conv_tail, conv_weight, conv_bias)
    projected = jnp.dot(mixed, x_weight, preferred_element_type=jnp.float32)
    rank_part = projected[:, :RANK].astype(jnp.bfloat16)
    delta = jax.nn.softplus(jnp.dot(rank_part, dt_weight, preferred_element_type=jnp.float32) + dt_bias[None, :])
    b_part = projected[:, RANK:RANK + STATE]
    c_part = projected[:, RANK + STATE:]
    readout, state_out = run_states(mixed, gate_in, delta, b_part, c_part, ssm_state, decay_log, skip_gain)
    blocks = readout.reshape(TOKENS, N_TENSOR, E_DEV).transpose(1, 0, 2)
    weight_blocks = out_weight.reshape(N_TENSOR, E_DEV, D)

    def add_block(total, pair):
        partial_value = jnp.dot(pair[0], pair[1], preferred_element_type=jnp.float32).astype(jnp.bfloat16)
        partial_value = lax.optimization_barrier(partial_value)
        return (total + partial_value.astype(jnp.float32), None)
    mixer, _ = lax.scan(add_block, jnp.zeros((TOKENS, D), jnp.float32), (blocks, weight_blocks))
    hidden_state = resid.astype(jnp.float32) + mixer
    normed, route_weight = route_inputs(hidden_state, expert_ids, norm_gain, router_weight)
    gated = jnp.dot(normed, w_gate, preferred_element_type=jnp.float32)
    upward = jnp.dot(normed, w_up, preferred_element_type=jnp.float32)
    expert_hidden = (jax.nn.silu(gated) * upward).astype(jnp.bfloat16)
    hidden_blocks = expert_hidden.reshape(TOKENS, N_TENSOR, FF_DEV).transpose(1, 0, 2)
    down_blocks = w_down.reshape(N_TENSOR, FF_DEV, D)
    expert_sum, _ = lax.scan(add_block, jnp.zeros((TOKENS, D), jnp.float32), (hidden_blocks, down_blocks))
    layer_out = (hidden_state + route_weight[:, None] * expert_sum).astype(jnp.bfloat16)
    return (layer_out, state_out)
```

```python
import jax
import jax.numpy as jnp
from jax import lax
from jax.experimental import pallas as pl
from jax.experimental.pallas import tpu as pltpu
from jax.sharding import PartitionSpec as P

RANK = 512
STATE = 16
CONV = 4
EXPERTS = 16
TOPK = 2
STEPS = 4
REQ = 128


EPSILON = 1e-06
MESH = pl.DeviceIdType.MESH


def radices(devices):
    chips = devices // 2
    outer = min(4, chips)
    return (outer, chips // outer, 2)


class Place:
    def __init__(self, devices):
        self.d2, self.d1, self.d0 = radices(devices)
        self.group = lax.axis_index("groups")
        me = lax.axis_index("tensor")
        self.i0 = lax.rem(me, self.d0)
        self.i1 = lax.rem(me // self.d0, self.d1)
        self.i2 = me // (self.d0 * self.d1)

    def digit(self, stage, step):
        now = (self.i0, self.i1, self.i2)[stage]
        radix = (self.d0, self.d1, self.d2)[stage]
        return lax.rem(now + step, radix)

    def device(self, stage, step):
        index = [self.i0, self.i1, self.i2]
        index[stage] = self.digit(stage, step)
        return (self.group, (index[2] * self.d1 + index[1]) * self.d0 + index[0])

    def barrier(self):
        semaphore = pltpu.get_barrier_semaphore()
        count = 0
        for stage, radix in enumerate((self.d0, self.d1, self.d2)):
            for step in range(1, radix):
                pl.semaphore_signal(
                    semaphore, inc=1, device_id=self.device(stage, step), device_id_type=MESH
                )
                count += 1
        pl.semaphore_wait(semaphore, count)


def send(source, target, send_sem, recv_sem, device):
    copy = pltpu.make_async_remote_copy(
        src_ref=source,
        dst_ref=target,
        send_sem=send_sem,
        recv_sem=recv_sem,
        device_id=device,
        device_id_type=MESH,
    )
    copy.start()
    return copy


def real(value):
    return value.astype(jnp.float32)


def reduce_parts(place, chunks, x_ref, finish, recv0, recv1, recv2, sems):
    d2, d1, d0 = place.d2, place.d1, place.d0
    width = x_ref.shape[-1] // chunks
    copies = []

    def columns(chunk):
        return slice(None) if chunks == 1 else pl.ds(chunk * width, width)

    def start0(chunk):
        return [
            send(
                x_ref.at[:, :, place.digit(0, step), :, columns(chunk)],
                recv0.at[chunk, step - 1],
                sems[0].at[chunk, step - 1],
                sems[1].at[chunk, step - 1],
                place.device(0, step),
            )
            for step in range(1, d0)
        ]

    def start1(chunk):
        def add(outer, carry):
            for inner in range(d1):
                total = real(x_ref[outer, inner, place.i0, :, columns(chunk)])
                for step in range(1, d0):
                    total = total + real(recv0[chunk, step - 1, outer, inner])
                recv0[chunk, 0, outer, inner] = total.astype(recv0.dtype)
            return carry

        lax.fori_loop(0, d2, add, 0)
        return [
            send(
                recv0.at[chunk, 0, :, place.digit(1, step)],
                recv1.at[chunk, step - 1],
                sems[2].at[chunk, step - 1],
                sems[3].at[chunk, step - 1],
                place.device(1, step),
            )
            for step in range(1, d1)
        ]

    def start2(chunk):
        def add(outer, carry):
            total = real(recv0[chunk, 0, outer, place.i1])
            for step in range(1, d1):
                total = total + real(recv1[chunk, step - 1, outer])
            recv1[chunk, 0, outer] = total.astype(recv1.dtype)
            return carry

        lax.fori_loop(0, d2, add, 0)
        return [
            send(
                recv1.at[chunk, 0, place.digit(2, step)],
                recv2.at[chunk, step - 1],
                sems[4].at[chunk, step - 1],
                sems[5].at[chunk, step - 1],
                place.device(2, step),
            )
            for step in range(1, d2)
        ]

    def last(chunk):
        total = real(recv1[chunk, 0, place.i2])
        for step in range(1, d2):
            total = total + real(recv2[chunk, step - 1])
        finish(chunk, columns(chunk), total)
        return []

    flying = {}
    for tick in range(chunks + 3):
        for stage, run in enumerate((start0, start1, start2, last)):
            chunk = tick - stage
            if 0 <= chunk < chunks:
                if stage:
                    for copy in flying[stage - 1, chunk]:
                        copy.wait_recv()
                flying[stage, chunk] = run(chunk)
                copies.extend(flying[stage, chunk])
    return copies


def gather_parts(place, chunks, out_ref, sems):
    d2, d1, d0 = place.d2, place.d1, place.d0
    width = out_ref.shape[-1] // chunks
    copies = []

    def columns(chunk):
        return slice(None) if chunks == 1 else pl.ds(chunk * width, width)

    def held(stage, chunk):
        if stage == 2:
            return out_ref.at[place.i2, place.i1, place.i0, :, columns(chunk)]
        if stage == 1:
            return out_ref.at[:, place.i1, place.i0, :, columns(chunk)]
        return out_ref.at[:, :, place.i0, :, columns(chunk)]

    order = ((2, d2), (1, d1), (0, d0))
    flying = {}
    for tick in range(chunks + len(order)):
        for spot in range(len(order) + 1):
            chunk = tick - spot
            if not 0 <= chunk < chunks:
                continue
            if spot:
                for copy in flying[spot - 1, chunk]:
                    copy.wait_recv()
            if spot < len(order):
                stage, radix = order[spot]
                flying[spot, chunk] = [
                    send(
                        held(stage, chunk),
                        held(stage, chunk),
                        sems[2 * stage].at[chunk, step - 1],
                        sems[2 * stage + 1].at[chunk, step - 1],
                        place.device(stage, step),
                    )
                    for step in range(1, radix)
                ]
                copies.extend(flying[spot, chunk])
    return copies


def sem_shapes(devices, chunks):
    d2, d1, d0 = radices(devices)
    shapes = []
    for radix in (d0, d1, d2):
        shapes += [pltpu.SemaphoreType.DMA((chunks, max(1, radix - 1)))] * 2
    return shapes


def recv_shapes(devices, chunks, rows, width):
    d2, d1, d0 = radices(devices)
    return [
        pltpu.VMEM((chunks, d0 - 1, d2, d1, rows, width), jnp.bfloat16),
        pltpu.VMEM((chunks, max(1, d1 - 1), d2, rows, width), jnp.bfloat16),
        pltpu.VMEM((chunks, max(1, d2 - 1), rows, width), jnp.bfloat16),
    ]


def params(number):
    return pltpu.CompilerParams(
        collective_id=number, has_side_effects=True, vmem_limit_bytes=56 * 1024 * 1024
    )


VMEM = pl.BlockSpec(memory_space=pltpu.VMEM)


def all_sum(x, devices, number):
    d2, d1, d0 = radices(devices)
    rows, width = x.shape[0] // devices, x.shape[1]

    def kernel(x_ref, out_ref, recv0, recv1, recv2, *sems):
        place = Place(devices)
        place.barrier()

        def finish(chunk, columns, total):
            out_ref[place.i2, place.i1, place.i0] = total.astype(out_ref.dtype)

        copies = reduce_parts(place, 1, x_ref, finish, recv0, recv1, recv2, sems[:6])
        copies += gather_parts(place, 1, out_ref, sems[6:])
        for copy in copies:
            copy.wait_send()

    out = pl.pallas_call(
        kernel,
        out_shape=jax.ShapeDtypeStruct((d2, d1, d0, rows, width), jnp.bfloat16),
        in_specs=[VMEM],
        out_specs=VMEM,
        scratch_shapes=recv_shapes(devices, 1, rows, width) + sem_shapes(devices, 1) * 2,
        compiler_params=params(number),
        name="all_sum",
    )(x.reshape(d2, d1, d0, rows, width))
    return out.reshape(x.shape)


def scatter_sum(x, devices, chunks, number):
    d2, d1, d0 = radices(devices)
    rows, width = x.shape[0] // devices, x.shape[1]

    def kernel(x_ref, out_ref, recv0, recv1, recv2, *sems):
        place = Place(devices)
        place.barrier()

        def finish(chunk, columns, total):
            out_ref[:, columns] = total

        copies = reduce_parts(place, chunks, x_ref, finish, recv0, recv1, recv2, sems)
        for copy in copies:
            copy.wait_send()

    return pl.pallas_call(
        kernel,
        out_shape=jax.ShapeDtypeStruct((rows, width), jnp.float32),
        in_specs=[VMEM],
        out_specs=VMEM,
        scratch_shapes=recv_shapes(devices, chunks, rows, width // chunks)
        + sem_shapes(devices, chunks),
        compiler_params=params(number),
        name="scatter_sum",
    )(x.reshape(d2, d1, d0, rows, width))


def gather(x, devices, chunks, number):
    d2, d1, d0 = radices(devices)
    rows, width = x.shape

    def kernel(x_ref, out_ref, *sems):
        place = Place(devices)
        out_ref[place.i2, place.i1, place.i0] = x_ref[...]
        place.barrier()
        for copy in gather_parts(place, chunks, out_ref, sems):
            copy.wait_send()

    out = pl.pallas_call(
        kernel,
        out_shape=jax.ShapeDtypeStruct((d2, d1, d0, rows, width), x.dtype),
        in_specs=[VMEM],
        out_specs=VMEM,
        scratch_shapes=sem_shapes(devices, chunks),
        compiler_params=params(number),
        name="gather",
    )(x)
    return out.reshape(devices * rows, width)


def convolve(mixer_in, conv_tail, conv_weight, conv_bias):
    width = mixer_in.shape[1]
    inputs = mixer_in.reshape(STEPS, REQ, width).astype(jnp.float32)
    history = jnp.concatenate([conv_tail.astype(jnp.float32), inputs], axis=0)
    kernel = conv_weight.astype(jnp.float32)
    summed = conv_bias[None, None, :] + kernel[0] * history[0:STEPS]
    for offset in range(1, CONV):
        summed = summed + kernel[offset] * history[offset : offset + STEPS]
    return jax.nn.silu(summed).astype(jnp.bfloat16).reshape(STEPS * REQ, width)


def run_states(mixed, gate_in, delta, b_part, c_part, ssm_state, decay_log, skip_gain):
    rate = -jnp.exp(decay_log)
    state = ssm_state.astype(jnp.float32)
    results = []
    for position in range(STEPS):
        first = position * REQ
        step_delta = delta[first : first + REQ]
        step_input = mixed[first : first + REQ].astype(jnp.float32)
        decay = jnp.exp(step_delta[:, None, :] * rate[None, :, :])
        state = (
            decay * state
            + (step_delta * step_input)[:, None, :] * b_part[first : first + REQ][:, :, None]
        )
        reading = (
            jnp.sum(c_part[first : first + REQ][:, :, None] * state, axis=1)
            + skip_gain[None, :] * step_input
        )
        results.append(reading * jax.nn.silu(gate_in[first : first + REQ].astype(jnp.float32)))
    return (jnp.concatenate(results, axis=0).astype(jnp.bfloat16), state.astype(jnp.bfloat16))


def route_inputs(hidden_state, expert_ids, norm_gain, router_weight):
    scale = lax.rsqrt(jnp.mean(hidden_state * hidden_state, axis=1, keepdims=True) + EPSILON)
    normed = (hidden_state * scale * norm_gain.astype(jnp.float32)[None, :]).astype(jnp.bfloat16)
    logits = jnp.dot(normed, router_weight, preferred_element_type=jnp.float32)
    labels = jnp.arange(logits.shape[1], dtype=jnp.int32)
    onehot = expert_ids[:, :, None] == labels[None, None, :]
    picked = jnp.sum(jnp.where(onehot, logits[:, None, :], 0.0), axis=2)
    weight_first = jax.nn.sigmoid(picked[:, 0] - picked[:, 1])
    weight_second = jax.nn.sigmoid(picked[:, 1] - picked[:, 0])
    route_weight = jnp.where(
        expert_ids[:, 0] == 0, weight_first, jnp.where(expert_ids[:, 1] == 0, weight_second, 0.0)
    )
    return (normed, route_weight)


def slot_matrix(own_ids, route_weight, most):
    member = jnp.logical_or(own_ids[:, 0] == 0, own_ids[:, 1] == 0).astype(jnp.int32)
    ranked = jnp.cumsum(member, dtype=jnp.int32) - member
    slots = jnp.arange(most, dtype=jnp.int32)
    choose = jnp.logical_and(member[None, :] > 0, ranked[None, :] == slots[:, None])
    choose_real = choose.astype(jnp.float32)
    return (choose_real, choose_real * route_weight[None, :])


def expert_hidden_rows(rows, w_gate, w_up):
    gated = jnp.dot(rows, w_gate, preferred_element_type=jnp.float32)
    upward = jnp.dot(rows, w_up, preferred_element_type=jnp.float32)
    return (jax.nn.silu(gated) * upward).astype(jnp.bfloat16)


def per_device(
    mixer_in,
    gate_in,
    conv_tail,
    ssm_state,
    resid,
    expert_ids,
    conv_weight,
    conv_bias,
    x_weight,
    dt_weight,
    dt_bias,
    decay_log,
    skip_gain,
    out_weight,
    norm_gain,
    router_weight,
    w_gate,
    w_up,
    w_down,
):
    devices = lax.axis_size("tensor")
    tokens_total = mixer_in.shape[0]
    own_count = tokens_total // devices
    most = max(2, own_count * TOPK * 3 // EXPERTS)
    most = (most + 15) // 16 * 16
    mixed = convolve(mixer_in, conv_tail, conv_weight, conv_bias)
    partial_proj = jnp.dot(mixed, x_weight, preferred_element_type=jnp.float32)
    projected = all_sum(partial_proj.astype(jnp.bfloat16), devices, 0).astype(jnp.float32)
    rank_part = projected[:, :RANK].astype(jnp.bfloat16)
    delta = jax.nn.softplus(
        jnp.dot(rank_part, dt_weight, preferred_element_type=jnp.float32) + dt_bias[None, :]
    )
    b_part = projected[:, RANK : RANK + STATE]
    c_part = projected[:, RANK + STATE :]
    readout, state_out = run_states(
        mixed, gate_in, delta, b_part, c_part, ssm_state, decay_log, skip_gain
    )
    position = lax.axis_index("tensor")
    piece = readout
    mixer_rows = scatter_sum(
        jnp.dot(piece, out_weight, preferred_element_type=jnp.float32).astype(jnp.bfloat16),
        devices,
        8,
        1,
    )
    own_ids = lax.dynamic_slice_in_dim(expert_ids, position * own_count, own_count, 0)
    hidden_state = resid.astype(jnp.float32) + mixer_rows
    normed, route_weight = route_inputs(hidden_state, own_ids, norm_gain, router_weight)
    choose_real, coefficient = slot_matrix(own_ids, route_weight, most)
    packed = jnp.dot(
        choose_real.astype(jnp.bfloat16), normed, preferred_element_type=jnp.float32
    ).astype(jnp.bfloat16)
    all_hidden = expert_hidden_rows(
        gather(packed, devices, 4, 2), w_gate, w_up
    )
    piece = all_hidden
    summed = scatter_sum(
        jnp.dot(piece, w_down, preferred_element_type=jnp.float32).astype(jnp.bfloat16),
        devices,
        4,
        3,
    )
    expert_rows = jnp.dot(coefficient.T, summed, precision=lax.Precision.HIGHEST)
    layer_out = (hidden_state + expert_rows).astype(jnp.bfloat16)
    return (layer_out, state_out)


def solution(mesh):
    return jax.shard_map(
        per_device,
        mesh=mesh,
        in_specs=(
            P("groups", "tensor"),
            P("groups", "tensor"),
            P(None, "groups", "tensor"),
            P("groups", None, "tensor"),
            P(("groups", "tensor"), None),
            P("groups", None),
            P(None, "tensor"),
            P("tensor"),
            P("tensor", None),
            P(None, "tensor"),
            P("tensor"),
            P(None, "tensor"),
            P("tensor"),
            P("tensor", None),
            P(),
            P(),
            P(None, "tensor"),
            P(None, "tensor"),
            P("tensor", None),
        ),
        out_specs=(P(("groups", "tensor"), None), P("groups", None, "tensor")),
        check_vma=False,
    )
```

```python
import jax
import jax.numpy as jnp
from jax import lax
from jax.experimental import pallas as pl
from jax.experimental.pallas import tpu as pltpu
from jax.sharding import PartitionSpec as P

RANK = 512
STATE = 16
CONV = 4
EXPERTS = 16
TOPK = 2
STEPS = 4
REQ = 128


EPSILON = 1e-06
MESH = pl.DeviceIdType.MESH


def radices(devices):
    chips = devices // 2
    outer = min(4, chips)
    return (outer, chips // outer, 2)


class Place:
    def __init__(self, devices):
        self.d2, self.d1, self.d0 = radices(devices)
        self.group = lax.axis_index("groups")
        me = lax.axis_index("tensor")
        self.i0 = lax.rem(me, self.d0)
        self.i1 = lax.rem(me // self.d0, self.d1)
        self.i2 = me // (self.d0 * self.d1)

    def digit(self, stage, step):
        now = (self.i0, self.i1, self.i2)[stage]
        radix = (self.d0, self.d1, self.d2)[stage]
        return lax.rem(now + step, radix)

    def device(self, stage, step):
        index = [self.i0, self.i1, self.i2]
        index[stage] = self.digit(stage, step)
        return (self.group, (index[2] * self.d1 + index[1]) * self.d0 + index[0])

    def barrier(self):
        semaphore = pltpu.get_barrier_semaphore()
        count = 0
        for stage, radix in enumerate((self.d0, self.d1, self.d2)):
            for step in range(1, radix):
                pl.semaphore_signal(
                    semaphore, inc=1, device_id=self.device(stage, step), device_id_type=MESH
                )
                count += 1
        pl.semaphore_wait(semaphore, count)


def send(source, target, send_sem, recv_sem, device):
    copy = pltpu.make_async_remote_copy(
        src_ref=source,
        dst_ref=target,
        send_sem=send_sem,
        recv_sem=recv_sem,
        device_id=device,
        device_id_type=MESH,
    )
    copy.start()
    return copy


def real(value):
    return value.astype(jnp.float32)


def reduce_parts(place, chunks, x_ref, produce, finish, recv0, recv1, recv2, sems):
    d2, d1, d0 = place.d2, place.d1, place.d0
    width = x_ref.shape[-1] // chunks
    copies = []

    def columns(chunk):
        return slice(None) if chunks == 1 else pl.ds(chunk * width, width)

    def start0(chunk):
        produce(chunk, columns(chunk))
        return [
            send(
                x_ref.at[:, :, place.digit(0, step), :, columns(chunk)],
                recv0.at[chunk, step - 1],
                sems[0].at[chunk, step - 1],
                sems[1].at[chunk, step - 1],
                place.device(0, step),
            )
            for step in range(1, d0)
        ]

    def start1(chunk):
        def add(outer, carry):
            for inner in range(d1):
                total = real(x_ref[outer, inner, place.i0, :, columns(chunk)])
                for step in range(1, d0):
                    total = total + real(recv0[chunk, step - 1, outer, inner])
                recv0[chunk, 0, outer, inner] = total.astype(recv0.dtype)
            return carry

        lax.fori_loop(0, d2, add, 0)
        return [
            send(
                recv0.at[chunk, 0, :, place.digit(1, step)],
                recv1.at[chunk, step - 1],
                sems[2].at[chunk, step - 1],
                sems[3].at[chunk, step - 1],
                place.device(1, step),
            )
            for step in range(1, d1)
        ]

    def start2(chunk):
        def add(outer, carry):
            total = real(recv0[chunk, 0, outer, place.i1])
            for step in range(1, d1):
                total = total + real(recv1[chunk, step - 1, outer])
            recv1[chunk, 0, outer] = total.astype(recv1.dtype)
            return carry

        lax.fori_loop(0, d2, add, 0)
        return [
            send(
                recv1.at[chunk, 0, place.digit(2, step)],
                recv2.at[chunk, step - 1],
                sems[4].at[chunk, step - 1],
                sems[5].at[chunk, step - 1],
                place.device(2, step),
            )
            for step in range(1, d2)
        ]

    def last(chunk):
        total = real(recv1[chunk, 0, place.i2])
        for step in range(1, d2):
            total = total + real(recv2[chunk, step - 1])
        finish(chunk, columns(chunk), total)
        return []

    def landed(group):
        for copy in group:
            copy.wait_recv()
        copies.extend(group)

    first, second = [], []
    for chunk in range(chunks + 1):
        if chunk < chunks:
            first.append(start0(chunk))
        if chunk > 0:
            landed(first[chunk - 1])
            second.append(start1(chunk - 1))
    third = []
    for chunk in range(chunks):
        landed(second[chunk])
        third.append(start2(chunk))
    for chunk in range(chunks):
        landed(third[chunk])
        last(chunk)
    return copies


def gather_parts(place, chunks, out_ref, use, sems):
    d2, d1, d0 = place.d2, place.d1, place.d0
    width = out_ref.shape[-1] // chunks
    copies = []

    def columns(chunk):
        return slice(None) if chunks == 1 else pl.ds(chunk * width, width)

    def held(stage, chunk):
        if stage == 2:
            return out_ref.at[place.i2, place.i1, place.i0, :, columns(chunk)]
        if stage == 1:
            return out_ref.at[:, place.i1, place.i0, :, columns(chunk)]
        return out_ref.at[:, :, place.i0, :, columns(chunk)]

    def start(stage, radix, chunk):
        return [
            send(
                held(stage, chunk),
                held(stage, chunk),
                sems[2 * stage].at[chunk, step - 1],
                sems[2 * stage + 1].at[chunk, step - 1],
                place.device(stage, step),
            )
            for step in range(1, radix)
        ]

    def landed(group):
        for copy in group:
            copy.wait_recv()
        copies.extend(group)

    first = [start(2, d2, chunk) for chunk in range(chunks)]
    second = []
    for chunk in range(chunks):
        landed(first[chunk])
        second.append(start(1, d1, chunk))
    third = []
    for chunk in range(chunks + 1):
        if chunk < chunks:
            landed(second[chunk])
            third.append(start(0, d0, chunk))
        if chunk > 0:
            landed(third[chunk - 1])
            use(chunk - 1, columns(chunk - 1))
    return copies


def sem_shapes(devices, chunks):
    d2, d1, d0 = radices(devices)
    shapes = []
    for radix in (d0, d1, d2):
        shapes += [pltpu.SemaphoreType.DMA((chunks, max(1, radix - 1)))] * 2
    return shapes


def recv_shapes(devices, chunks, rows, width):
    d2, d1, d0 = radices(devices)
    return [
        pltpu.VMEM((chunks, d0 - 1, d2, d1, rows, width), jnp.bfloat16),
        pltpu.VMEM((chunks, max(1, d1 - 1), d2, rows, width), jnp.bfloat16),
        pltpu.VMEM((chunks, max(1, d2 - 1), rows, width), jnp.bfloat16),
    ]


def params(number, mebibytes):
    return pltpu.CompilerParams(
        collective_id=number, has_side_effects=True, vmem_limit_bytes=mebibytes * 1024 * 1024
    )


def nothing(chunk, columns):
    return None


VMEM = pl.BlockSpec(memory_space=pltpu.VMEM)


def all_sum(x, devices, number):
    d2, d1, d0 = radices(devices)
    rows, width = x.shape[0] // devices, x.shape[1]

    def kernel(x_ref, out_ref, recv0, recv1, recv2, *sems):
        place = Place(devices)
        place.barrier()

        def finish(chunk, columns, total):
            out_ref[place.i2, place.i1, place.i0] = total.astype(out_ref.dtype)

        copies = reduce_parts(place, 1, x_ref, nothing, finish, recv0, recv1, recv2, sems[:6])
        copies += gather_parts(place, 1, out_ref, nothing, sems[6:])
        for copy in copies:
            copy.wait_send()

    out = pl.pallas_call(
        kernel,
        out_shape=jax.ShapeDtypeStruct((d2, d1, d0, rows, width), jnp.bfloat16),
        in_specs=[VMEM],
        out_specs=VMEM,
        scratch_shapes=recv_shapes(devices, 1, rows, width) + sem_shapes(devices, 1) * 2,
        compiler_params=params(number, 8),
        name="all_sum",
    )(x.reshape(d2, d1, d0, rows, width))
    return out.reshape(x.shape)


def project_scatter(piece, weight, devices, chunks, number):
    d2, d1, d0 = radices(devices)
    rows, width = piece.shape[0] // devices, weight.shape[1]

    def kernel(piece_ref, weight_ref, out_ref, x_ref, recv0, recv1, recv2, *sems):
        place = Place(devices)
        place.barrier()

        def produce(chunk, columns):
            part = jnp.dot(
                piece_ref[...], weight_ref[:, columns], preferred_element_type=jnp.float32
            ).astype(jnp.bfloat16)
            x_ref[:, :, :, :, columns] = part.reshape(d2, d1, d0, rows, width // chunks)

        def finish(chunk, columns, total):
            out_ref[:, columns] = total

        copies = reduce_parts(place, chunks, x_ref, produce, finish, recv0, recv1, recv2, sems)
        for copy in copies:
            copy.wait_send()

    return pl.pallas_call(
        kernel,
        out_shape=jax.ShapeDtypeStruct((rows, width), jnp.float32),
        in_specs=[VMEM, VMEM],
        out_specs=VMEM,
        scratch_shapes=[pltpu.VMEM((d2, d1, d0, rows, width), jnp.bfloat16)]
        + recv_shapes(devices, chunks, rows, width // chunks)
        + sem_shapes(devices, chunks),
        compiler_params=params(number, 40),
        name="project_scatter",
    )(piece, weight)


def run_expert(packed, w_gate, w_up, w_down, devices, chunks, number):
    d2, d1, d0 = radices(devices)
    rows, width = packed.shape
    units = w_gate.shape[1]
    tokens = devices * rows

    def kernel(
        packed_ref, gate_ref, up_ref, down_ref, out_ref,
        all_ref, x_ref, both_ref, lower_ref, sum_ref, hidden_ref, load_sems, recv0, recv1, recv2, *sems
    ):
        loads = [
            pltpu.make_async_copy(gate_ref, both_ref.at[:, pl.ds(0, units)], load_sems.at[0]),
            pltpu.make_async_copy(up_ref, both_ref.at[:, pl.ds(units, units)], load_sems.at[1]),
            pltpu.make_async_copy(down_ref, lower_ref, load_sems.at[2]),
        ]
        for load in loads:
            load.start()
        place = Place(devices)
        all_ref[place.i2, place.i1, place.i0] = packed_ref[...]
        place.barrier()

        def use(chunk, columns):
            if chunk == 0:
                loads[0].wait()
                loads[1].wait()
            part = jnp.dot(
                all_ref[:, :, :, :, columns].reshape(tokens, width // chunks),
                both_ref[columns, :],
                preferred_element_type=jnp.float32,
            )
            if chunk == 0:
                sum_ref[...] = part
            else:
                sum_ref[...] += part

        copies = gather_parts(place, chunks, all_ref, use, sems[:6])
        hidden_ref[...] = (jax.nn.silu(sum_ref[:, :units]) * sum_ref[:, units:]).astype(jnp.bfloat16)
        loads[2].wait()

        def produce(chunk, columns):
            part = jnp.dot(
                hidden_ref[...], lower_ref[:, columns], preferred_element_type=jnp.float32
            ).astype(jnp.bfloat16)
            x_ref[:, :, :, :, columns] = part.reshape(d2, d1, d0, rows, width // chunks)

        def finish(chunk, columns, total):
            out_ref[:, columns] = total

        copies += reduce_parts(
            place, chunks, x_ref, produce, finish, recv0, recv1, recv2, sems[6:]
        )
        for copy in copies:
            copy.wait_send()

    return pl.pallas_call(
        kernel,
        out_shape=jax.ShapeDtypeStruct((rows, width), jnp.float32),
        in_specs=[VMEM] + [pl.BlockSpec(memory_space=pl.ANY)] * 3,
        out_specs=VMEM,
        scratch_shapes=[
            pltpu.VMEM((d2, d1, d0, rows, width), jnp.bfloat16),
            pltpu.VMEM((d2, d1, d0, rows, width), jnp.bfloat16),
            pltpu.VMEM((width, 2 * units), jnp.bfloat16),
            pltpu.VMEM((units, width), jnp.bfloat16),
            pltpu.VMEM((tokens, 2 * units), jnp.float32),
            pltpu.VMEM((tokens, units), jnp.bfloat16),
            pltpu.SemaphoreType.DMA((3,)),
        ]
        + recv_shapes(devices, chunks, rows, width // chunks)
        + sem_shapes(devices, chunks) * 2,
        compiler_params=params(number, 56),
        name="run_expert",
    )(packed, w_gate, w_up, w_down)


def convolve(mixer_in, conv_tail, conv_weight, conv_bias):
    width = mixer_in.shape[1]
    inputs = mixer_in.reshape(STEPS, REQ, width).astype(jnp.float32)
    history = jnp.concatenate([conv_tail.astype(jnp.float32), inputs], axis=0)
    kernel = conv_weight.astype(jnp.float32)
    summed = conv_bias[None, None, :] + kernel[0] * history[0:STEPS]
    for offset in range(1, CONV):
        summed = summed + kernel[offset] * history[offset : offset + STEPS]
    return jax.nn.silu(summed).astype(jnp.bfloat16).reshape(STEPS * REQ, width)


def run_states(mixed, gate_in, delta, b_part, c_part, ssm_state, decay_log, skip_gain):
    rate = -jnp.exp(decay_log)
    state = ssm_state.astype(jnp.float32)
    results = []
    for position in range(STEPS):
        first = position * REQ
        step_delta = delta[first : first + REQ]
        step_input = mixed[first : first + REQ].astype(jnp.float32)
        decay = jnp.exp(step_delta[:, None, :] * rate[None, :, :])
        state = (
            decay * state
            + (step_delta * step_input)[:, None, :] * b_part[first : first + REQ][:, :, None]
        )
        reading = (
            jnp.sum(c_part[first : first + REQ][:, :, None] * state, axis=1)
            + skip_gain[None, :] * step_input
        )
        results.append(reading * jax.nn.silu(gate_in[first : first + REQ].astype(jnp.float32)))
    return (jnp.concatenate(results, axis=0).astype(jnp.bfloat16), state.astype(jnp.bfloat16))


def route_inputs(hidden_state, expert_ids, norm_gain, router_weight):
    scale = lax.rsqrt(jnp.mean(hidden_state * hidden_state, axis=1, keepdims=True) + EPSILON)
    normed = (hidden_state * scale * norm_gain.astype(jnp.float32)[None, :]).astype(jnp.bfloat16)
    logits = jnp.dot(normed, router_weight, preferred_element_type=jnp.float32)
    labels = jnp.arange(logits.shape[1], dtype=jnp.int32)
    onehot = expert_ids[:, :, None] == labels[None, None, :]
    picked = jnp.sum(jnp.where(onehot, logits[:, None, :], 0.0), axis=2)
    weight_first = jax.nn.sigmoid(picked[:, 0] - picked[:, 1])
    weight_second = jax.nn.sigmoid(picked[:, 1] - picked[:, 0])
    route_weight = jnp.where(
        expert_ids[:, 0] == 0, weight_first, jnp.where(expert_ids[:, 1] == 0, weight_second, 0.0)
    )
    return (normed, route_weight)


def slot_matrix(own_ids, route_weight, most):
    member = jnp.logical_or(own_ids[:, 0] == 0, own_ids[:, 1] == 0).astype(jnp.int32)
    ranked = jnp.cumsum(member, dtype=jnp.int32) - member
    slots = jnp.arange(most, dtype=jnp.int32)
    choose = jnp.logical_and(member[None, :] > 0, ranked[None, :] == slots[:, None])
    choose_real = choose.astype(jnp.float32)
    return (choose_real, choose_real * route_weight[None, :])


def per_device(
    mixer_in,
    gate_in,
    conv_tail,
    ssm_state,
    resid,
    expert_ids,
    conv_weight,
    conv_bias,
    x_weight,
    dt_weight,
    dt_bias,
    decay_log,
    skip_gain,
    out_weight,
    norm_gain,
    router_weight,
    w_gate,
    w_up,
    w_down,
):
    devices = lax.axis_size("tensor")
    tokens_total = mixer_in.shape[0]
    own_count = tokens_total // devices
    most = max(2, own_count * TOPK * 3 // EXPERTS)
    most = (most + 15) // 16 * 16
    mixed = convolve(mixer_in, conv_tail, conv_weight, conv_bias)
    partial_proj = jnp.dot(mixed, x_weight, preferred_element_type=jnp.float32)
    projected = all_sum(partial_proj.astype(jnp.bfloat16), devices, 0).astype(jnp.float32)
    rank_part = projected[:, :RANK].astype(jnp.bfloat16)
    delta = jax.nn.softplus(
        jnp.dot(rank_part, dt_weight, preferred_element_type=jnp.float32) + dt_bias[None, :]
    )
    b_part = projected[:, RANK : RANK + STATE]
    c_part = projected[:, RANK + STATE :]
    readout, state_out = run_states(
        mixed, gate_in, delta, b_part, c_part, ssm_state, decay_log, skip_gain
    )
    position = lax.axis_index("tensor")
    mixer_rows = project_scatter(readout, out_weight, devices, 16, 1)
    own_ids = lax.dynamic_slice_in_dim(expert_ids, position * own_count, own_count, 0)
    hidden_state = resid.astype(jnp.float32) + mixer_rows
    normed, route_weight = route_inputs(hidden_state, own_ids, norm_gain, router_weight)
    choose_real, coefficient = slot_matrix(own_ids, route_weight, most)
    packed = jnp.dot(
        choose_real.astype(jnp.bfloat16), normed, preferred_element_type=jnp.float32
    ).astype(jnp.bfloat16)
    summed = run_expert(packed, w_gate, w_up, w_down, devices, 8, 2)
    expert_rows = jnp.dot(coefficient.T, summed, precision=lax.Precision.HIGHEST)
    layer_out = (hidden_state + expert_rows).astype(jnp.bfloat16)
    return (layer_out, state_out)


def solution(mesh):
    return jax.shard_map(
        per_device,
        mesh=mesh,
        in_specs=(
            P("groups", "tensor"),
            P("groups", "tensor"),
            P(None, "groups", "tensor"),
            P("groups", None, "tensor"),
            P(("groups", "tensor"), None),
            P("groups", None),
            P(None, "tensor"),
            P("tensor"),
            P("tensor", None),
            P(None, "tensor"),
            P("tensor"),
            P(None, "tensor"),
            P("tensor"),
            P("tensor", None),
            P(),
            P(),
            P(None, "tensor"),
            P(None, "tensor"),
            P("tensor", None),
        ),
        out_specs=(P(("groups", "tensor"), None), P("groups", None, "tensor")),
        check_vma=False,
    )
```

```python
import itertools

import jax
import jax.numpy as jnp
from jax import lax
from jax.experimental import pallas as pl
from jax.experimental.pallas import tpu as pltpu
from jax.sharding import PartitionSpec as P

RANK = 512
STATE = 16
CONV = 4
EXPERTS = 16
TOPK = 2
STEPS = 4
REQ = 128


EPSILON = 1e-06
MESH = pl.DeviceIdType.MESH


def radices(devices, widest):
    chips = devices // 2
    digits = [2]
    if chips % 4:
        digits.append(chips)
        return digits
    while chips > 1:
        radix = 2 if chips == 8 else min(widest, chips)
        digits.append(radix)
        chips //= radix
    return digits


class Place:
    def __init__(self, digits):
        self.digits = digits
        self.group = lax.axis_index("groups")
        rest = lax.axis_index("tensor")
        self.own = []
        for radix in digits:
            self.own.append(lax.rem(rest, radix))
            rest = rest // radix

    def digit(self, stage, step):
        return lax.rem(self.own[stage] + step, self.digits[stage])

    def device(self, stage, step):
        index = 0
        for place in reversed(range(len(self.digits))):
            now = self.digit(place, step) if place == stage else self.own[place]
            index = index * self.digits[place] + now
        return (self.group, index)

    def block(self):
        return tuple(reversed(self.own))

    def barrier(self):
        semaphore = pltpu.get_barrier_semaphore()
        count = 0
        for stage, radix in enumerate(self.digits):
            for step in range(1, radix):
                pl.semaphore_signal(
                    semaphore, inc=1, device_id=self.device(stage, step), device_id_type=MESH
                )
                count += 1
        pl.semaphore_wait(semaphore, count)


def send(source, target, send_sem, recv_sem, device):
    copy = pltpu.make_async_remote_copy(
        src_ref=source,
        dst_ref=target,
        send_sem=send_sem,
        recv_sem=recv_sem,
        device_id=device,
        device_id_type=MESH,
    )
    copy.start()
    return copy


def real(value):
    return value.astype(jnp.float32)


def wait_landed(group):
    for copy in group:
        copy.wait_recv()


def reduce_parts(place, chunks, x_ref, produce, finish, recvs, sems):
    digits = place.digits
    stages = len(digits)
    width = x_ref.shape[-1] // chunks

    def columns(chunk):
        return slice(None) if chunks == 1 else pl.ds(chunk * width, width)

    def held(stage, chunk, index):
        if stage == 0:
            return x_ref.at[index + (slice(None), columns(chunk))]
        return recvs[stage - 1].at[(chunk, 0) + index]

    def start(stage, chunk):
        outer = (slice(None),) * (stages - 1 - stage)
        return [
            send(
                held(stage, chunk, outer + (place.digit(stage, step),)),
                recvs[stage].at[chunk, step - 1],
                sems[2 * stage].at[chunk, step - 1],
                sems[2 * stage + 1].at[chunk, step - 1],
                place.device(stage, step),
            )
            for step in range(1, digits[stage])
        ]

    def add(stage, chunk):
        recv = recvs[stage]
        for outer in itertools.product(*map(range, reversed(digits[stage + 1 :]))):
            total = real(held(stage, chunk, outer + (place.own[stage],))[...])
            for step in range(1, digits[stage]):
                total = total + real(recv[(chunk, step - 1) + outer])
            if stage == stages - 1:
                finish(chunk, columns(chunk), total)
            else:
                recv[(chunk, 0) + outer] = total.astype(recv.dtype)

    copies, flying, following = [], [], []
    for chunk in range(chunks + 1):
        if chunk < chunks:
            produce(chunk, columns(chunk))
            flying.append(start(0, chunk))
        if chunk > 0:
            wait_landed(flying[chunk - 1])
            add(0, chunk - 1)
            following.append(start(1, chunk - 1))
    for stage in range(1, stages):
        copies += flying
        flying, following = following, []
        for chunk in range(chunks):
            wait_landed(flying[chunk])
            add(stage, chunk)
            if stage + 1 < stages:
                following.append(start(stage + 1, chunk))
    copies += flying
    return [copy for group in copies for copy in group]


def gather_parts(place, chunks, out_ref, use, sems):
    stages = len(place.digits)
    width = out_ref.shape[-1] // chunks

    def columns(chunk):
        return slice(None) if chunks == 1 else pl.ds(chunk * width, width)

    def start(stage, chunk):
        index = (slice(None),) * (stages - 1 - stage) + place.block()[stages - 1 - stage :]
        held = out_ref.at[index + (slice(None), columns(chunk))]
        return [
            send(
                held,
                held,
                sems[2 * stage].at[chunk, step - 1],
                sems[2 * stage + 1].at[chunk, step - 1],
                place.device(stage, step),
            )
            for step in range(1, place.digits[stage])
        ]

    copies = []
    flying = [start(stages - 1, chunk) for chunk in range(chunks)]
    for stage in reversed(range(1, stages - 1)):
        copies += flying
        following = []
        for chunk in range(chunks):
            wait_landed(flying[chunk])
            following.append(start(stage, chunk))
        flying = following
    copies += flying
    last = []
    for chunk in range(chunks + 1):
        if chunk < chunks:
            wait_landed(flying[chunk])
            last.append(start(0, chunk))
        if chunk > 0:
            wait_landed(last[chunk - 1])
            use(chunk - 1, columns(chunk - 1))
    copies += last
    return [copy for group in copies for copy in group]


def sem_shapes(digits, chunks):
    shapes = []
    for radix in digits:
        shapes += [pltpu.SemaphoreType.DMA((chunks, radix - 1))] * 2
    return shapes


def recv_shapes(digits, chunks, rows, width):
    return [
        pltpu.VMEM(
            (chunks, radix - 1) + tuple(reversed(digits[stage + 1 :])) + (rows, width), jnp.bfloat16
        )
        for stage, radix in enumerate(digits)
    ]


def params(number, mebibytes):
    return pltpu.CompilerParams(
        collective_id=number, has_side_effects=True, vmem_limit_bytes=mebibytes * 1024 * 1024
    )


def nothing(chunk, columns):
    return None


VMEM = pl.BlockSpec(memory_space=pltpu.VMEM)


def all_sum(x, devices, number):
    digits = radices(devices, 4)
    count = len(digits)
    shape = tuple(reversed(digits))
    rows, width = x.shape[0] // devices, x.shape[1]

    def kernel(x_ref, out_ref, *scratch):
        recvs, sems = scratch[:count], scratch[count:]
        place = Place(digits)
        place.barrier()

        def finish(chunk, columns, total):
            out_ref[place.block()] = total.astype(out_ref.dtype)

        copies = reduce_parts(place, 1, x_ref, nothing, finish, recvs, sems[: 2 * count])
        copies += gather_parts(place, 1, out_ref, nothing, sems[2 * count :])
        for copy in copies:
            copy.wait_send()

    out = pl.pallas_call(
        kernel,
        out_shape=jax.ShapeDtypeStruct(shape + (rows, width), jnp.bfloat16),
        in_specs=[VMEM],
        out_specs=VMEM,
        scratch_shapes=recv_shapes(digits, 1, rows, width) + sem_shapes(digits, 1) * 2,
        compiler_params=params(number, 8),
        name="all_sum",
    )(x.reshape(shape + (rows, width)))
    return out.reshape(x.shape)


def project_scatter(piece, weight, devices, chunks, number):
    digits = radices(devices, 2)
    count = len(digits)
    shape = tuple(reversed(digits))
    rows, width = piece.shape[0] // devices, weight.shape[1]

    def kernel(piece_ref, weight_ref, out_ref, x_ref, *scratch):
        recvs, sems = scratch[:count], scratch[count:]
        place = Place(digits)
        place.barrier()

        def produce(chunk, columns):
            part = jnp.dot(
                piece_ref[...], weight_ref[:, columns], preferred_element_type=jnp.float32
            ).astype(jnp.bfloat16)
            x_ref[(slice(None),) * (count + 1) + (columns,)] = part.reshape(
                shape + (rows, width // chunks)
            )

        def finish(chunk, columns, total):
            out_ref[:, columns] = total

        copies = reduce_parts(place, chunks, x_ref, produce, finish, recvs, sems)
        for copy in copies:
            copy.wait_send()

    return pl.pallas_call(
        kernel,
        out_shape=jax.ShapeDtypeStruct((rows, width), jnp.float32),
        in_specs=[VMEM, VMEM],
        out_specs=VMEM,
        scratch_shapes=[pltpu.VMEM(shape + (rows, width), jnp.bfloat16)]
        + recv_shapes(digits, chunks, rows, width // chunks)
        + sem_shapes(digits, chunks),
        compiler_params=params(number, 40),
        name="project_scatter",
    )(piece, weight)


def run_expert(packed, w_gate, w_up, w_down, devices, chunks, number):
    digits = radices(devices, 2)
    count = len(digits)
    shape = tuple(reversed(digits))
    rows, width = packed.shape
    units = w_gate.shape[1]
    tokens = devices * rows

    def kernel(
        packed_ref, gate_ref, up_ref, down_ref, out_ref,
        all_ref, x_ref, both_ref, lower_ref, sum_ref, hidden_ref, load_sems, *scratch
    ):
        recvs, sems = scratch[:count], scratch[count:]
        loads = [
            pltpu.make_async_copy(gate_ref, both_ref.at[:, pl.ds(0, units)], load_sems.at[0]),
            pltpu.make_async_copy(up_ref, both_ref.at[:, pl.ds(units, units)], load_sems.at[1]),
            pltpu.make_async_copy(down_ref, lower_ref, load_sems.at[2]),
        ]
        for load in loads:
            load.start()
        place = Place(digits)
        all_ref[place.block()] = packed_ref[...]
        place.barrier()

        def use(chunk, columns):
            if chunk == 0:
                loads[0].wait()
                loads[1].wait()
            part = jnp.dot(
                all_ref[(slice(None),) * (count + 1) + (columns,)].reshape(tokens, width // chunks),
                both_ref[columns, :],
                preferred_element_type=jnp.float32,
            )
            if chunk == 0:
                sum_ref[...] = part
            else:
                sum_ref[...] += part

        copies = gather_parts(place, chunks, all_ref, use, sems[: 2 * count])
        hidden_ref[...] = (jax.nn.silu(sum_ref[:, :units]) * sum_ref[:, units:]).astype(jnp.bfloat16)
        loads[2].wait()

        def produce(chunk, columns):
            part = jnp.dot(
                hidden_ref[...], lower_ref[:, columns], preferred_element_type=jnp.float32
            ).astype(jnp.bfloat16)
            x_ref[(slice(None),) * (count + 1) + (columns,)] = part.reshape(
                shape + (rows, width // chunks)
            )

        def finish(chunk, columns, total):
            out_ref[:, columns] = total

        copies += reduce_parts(
            place, chunks, x_ref, produce, finish, recvs, sems[2 * count :]
        )
        for copy in copies:
            copy.wait_send()

    return pl.pallas_call(
        kernel,
        out_shape=jax.ShapeDtypeStruct((rows, width), jnp.float32),
        in_specs=[VMEM] + [pl.BlockSpec(memory_space=pl.ANY)] * 3,
        out_specs=VMEM,
        scratch_shapes=[
            pltpu.VMEM(shape + (rows, width), jnp.bfloat16),
            pltpu.VMEM(shape + (rows, width), jnp.bfloat16),
            pltpu.VMEM((width, 2 * units), jnp.bfloat16),
            pltpu.VMEM((units, width), jnp.bfloat16),
            pltpu.VMEM((tokens, 2 * units), jnp.float32),
            pltpu.VMEM((tokens, units), jnp.bfloat16),
            pltpu.SemaphoreType.DMA((3,)),
        ]
        + recv_shapes(digits, chunks, rows, width // chunks)
        + sem_shapes(digits, chunks) * 2,
        compiler_params=params(number, 56),
        name="run_expert",
    )(packed, w_gate, w_up, w_down)


def convolve(mixer_in, conv_tail, conv_weight, conv_bias):
    width = mixer_in.shape[1]
    inputs = mixer_in.reshape(STEPS, REQ, width).astype(jnp.float32)
    history = jnp.concatenate([conv_tail.astype(jnp.float32), inputs], axis=0)
    kernel = conv_weight.astype(jnp.float32)
    summed = conv_bias[None, None, :] + kernel[0] * history[0:STEPS]
    for offset in range(1, CONV):
        summed = summed + kernel[offset] * history[offset : offset + STEPS]
    return jax.nn.silu(summed).astype(jnp.bfloat16).reshape(STEPS * REQ, width)


def run_states(mixed, gate_in, delta, b_part, c_part, ssm_state, decay_log, skip_gain):
    rate = -jnp.exp(decay_log)
    state = ssm_state.astype(jnp.float32)
    results = []
    for position in range(STEPS):
        first = position * REQ
        step_delta = delta[first : first + REQ]
        step_input = mixed[first : first + REQ].astype(jnp.float32)
        decay = jnp.exp(step_delta[:, None, :] * rate[None, :, :])
        state = (
            decay * state
            + (step_delta * step_input)[:, None, :] * b_part[first : first + REQ][:, :, None]
        )
        reading = (
            jnp.sum(c_part[first : first + REQ][:, :, None] * state, axis=1)
            + skip_gain[None, :] * step_input
        )
        results.append(reading * jax.nn.silu(gate_in[first : first + REQ].astype(jnp.float32)))
    return (jnp.concatenate(results, axis=0).astype(jnp.bfloat16), state.astype(jnp.bfloat16))


def route_inputs(hidden_state, expert_ids, norm_gain, router_weight):
    scale = lax.rsqrt(jnp.mean(hidden_state * hidden_state, axis=1, keepdims=True) + EPSILON)
    normed = (hidden_state * scale * norm_gain.astype(jnp.float32)[None, :]).astype(jnp.bfloat16)
    logits = jnp.dot(normed, router_weight, preferred_element_type=jnp.float32)
    labels = jnp.arange(logits.shape[1], dtype=jnp.int32)
    onehot = expert_ids[:, :, None] == labels[None, None, :]
    picked = jnp.sum(jnp.where(onehot, logits[:, None, :], 0.0), axis=2)
    weight_first = jax.nn.sigmoid(picked[:, 0] - picked[:, 1])
    weight_second = jax.nn.sigmoid(picked[:, 1] - picked[:, 0])
    route_weight = jnp.where(
        expert_ids[:, 0] == 0, weight_first, jnp.where(expert_ids[:, 1] == 0, weight_second, 0.0)
    )
    return (normed, route_weight)


def slot_matrix(own_ids, route_weight, most):
    member = jnp.logical_or(own_ids[:, 0] == 0, own_ids[:, 1] == 0).astype(jnp.int32)
    ranked = jnp.cumsum(member, dtype=jnp.int32) - member
    slots = jnp.arange(most, dtype=jnp.int32)
    choose = jnp.logical_and(member[None, :] > 0, ranked[None, :] == slots[:, None])
    choose_real = choose.astype(jnp.float32)
    return (choose_real, choose_real * route_weight[None, :])


def per_device(
    mixer_in,
    gate_in,
    conv_tail,
    ssm_state,
    resid,
    expert_ids,
    conv_weight,
    conv_bias,
    x_weight,
    dt_weight,
    dt_bias,
    decay_log,
    skip_gain,
    out_weight,
    norm_gain,
    router_weight,
    w_gate,
    w_up,
    w_down,
):
    devices = lax.axis_size("tensor")
    tokens_total = mixer_in.shape[0]
    own_count = tokens_total // devices
    most = max(2, own_count * TOPK * 3 // EXPERTS)
    most = (most + 15) // 16 * 16
    mixed = convolve(mixer_in, conv_tail, conv_weight, conv_bias)
    partial_proj = jnp.dot(mixed, x_weight, preferred_element_type=jnp.float32)
    projected = all_sum(partial_proj.astype(jnp.bfloat16), devices, 0).astype(jnp.float32)
    rank_part = projected[:, :RANK].astype(jnp.bfloat16)
    delta = jax.nn.softplus(
        jnp.dot(rank_part, dt_weight, preferred_element_type=jnp.float32) + dt_bias[None, :]
    )
    b_part = projected[:, RANK : RANK + STATE]
    c_part = projected[:, RANK + STATE :]
    readout, state_out = run_states(
        mixed, gate_in, delta, b_part, c_part, ssm_state, decay_log, skip_gain
    )
    position = lax.axis_index("tensor")
    mixer_rows = project_scatter(readout, out_weight, devices, 16, 1)
    own_ids = lax.dynamic_slice_in_dim(expert_ids, position * own_count, own_count, 0)
    hidden_state = resid.astype(jnp.float32) + mixer_rows
    normed, route_weight = route_inputs(hidden_state, own_ids, norm_gain, router_weight)
    choose_real, coefficient = slot_matrix(own_ids, route_weight, most)
    packed = jnp.dot(
        choose_real.astype(jnp.bfloat16), normed, preferred_element_type=jnp.float32
    ).astype(jnp.bfloat16)
    summed = run_expert(packed, w_gate, w_up, w_down, devices, 8, 2)
    expert_rows = jnp.dot(coefficient.T, summed, precision=lax.Precision.HIGHEST)
    layer_out = (hidden_state + expert_rows).astype(jnp.bfloat16)
    return (layer_out, state_out)


def solution(mesh):
    return jax.shard_map(
        per_device,
        mesh=mesh,
        in_specs=(
            P("groups", "tensor"),
            P("groups", "tensor"),
            P(None, "groups", "tensor"),
            P("groups", None, "tensor"),
            P(("groups", "tensor"), None),
            P("groups", None),
            P(None, "tensor"),
            P("tensor"),
            P("tensor", None),
            P(None, "tensor"),
            P("tensor"),
            P(None, "tensor"),
            P("tensor"),
            P("tensor", None),
            P(),
            P(),
            P(None, "tensor"),
            P(None, "tensor"),
            P("tensor", None),
        ),
        out_specs=(P(("groups", "tensor"), None), P("groups", None, "tensor")),
        check_vma=False,
    )
```

```python
import itertools

import jax
import jax.numpy as jnp
from jax import lax
from jax.experimental import pallas as pl
from jax.experimental.pallas import tpu as pltpu
from jax.sharding import PartitionSpec as P

RANK = 512
STATE = 16
CONV = 4
EXPERTS = 16
TOPK = 2
STEPS = 4
REQ = 128


EPSILON = 1e-06
MESH = pl.DeviceIdType.MESH


def radices(devices, widest):
    chips = devices // 2
    digits = [2]
    if chips % 4:
        digits.append(chips)
        return digits
    while chips > 1:
        radix = 2 if chips == 8 else min(widest, chips)
        digits.append(radix)
        chips //= radix
    return digits


class Place:
    def __init__(self, digits):
        self.digits = digits
        self.group = lax.axis_index("groups")
        rest = lax.axis_index("tensor")
        self.own = []
        for radix in digits:
            self.own.append(lax.rem(rest, radix))
            rest = rest // radix

    def digit(self, stage, step):
        return lax.rem(self.own[stage] + step, self.digits[stage])

    def device(self, stage, step):
        index = 0
        for place in reversed(range(len(self.digits))):
            now = self.digit(place, step) if place == stage else self.own[place]
            index = index * self.digits[place] + now
        return (self.group, index)

    def block(self):
        return tuple(reversed(self.own))

    def barrier(self):
        semaphore = pltpu.get_barrier_semaphore()
        count = 0
        for stage, radix in enumerate(self.digits):
            for step in range(1, radix):
                pl.semaphore_signal(
                    semaphore, inc=1, device_id=self.device(stage, step), device_id_type=MESH
                )
                count += 1
        pl.semaphore_wait(semaphore, count)


def send(source, target, send_sem, recv_sem, device):
    copy = pltpu.make_async_remote_copy(
        src_ref=source,
        dst_ref=target,
        send_sem=send_sem,
        recv_sem=recv_sem,
        device_id=device,
        device_id_type=MESH,
    )
    copy.start()
    return copy


def real(value):
    return value.astype(jnp.float32)


def wait_landed(group):
    for copy in group:
        copy.wait_recv()


def reduce_parts(place, chunks, x_ref, produce, finish, recvs, sems):
    digits = place.digits
    stages = len(digits)
    width = x_ref.shape[-1] // chunks

    def columns(chunk):
        return slice(None) if chunks == 1 else pl.ds(chunk * width, width)

    def held(stage, chunk, index):
        if stage == 0:
            return x_ref.at[index + (slice(None), columns(chunk))]
        return recvs[stage - 1].at[(chunk, 0) + index]

    def start(stage, chunk):
        outer = (slice(None),) * (stages - 1 - stage)
        return [
            send(
                held(stage, chunk, outer + (place.digit(stage, step),)),
                recvs[stage].at[chunk, step - 1],
                sems[2 * stage].at[chunk, step - 1],
                sems[2 * stage + 1].at[chunk, step - 1],
                place.device(stage, step),
            )
            for step in range(1, digits[stage])
        ]

    def add(stage, chunk):
        recv = recvs[stage]
        for outer in itertools.product(*map(range, reversed(digits[stage + 1 :]))):
            total = real(held(stage, chunk, outer + (place.own[stage],))[...])
            for step in range(1, digits[stage]):
                total = total + real(recv[(chunk, step - 1) + outer])
            if stage == stages - 1:
                finish(chunk, columns(chunk), total)
            else:
                recv[(chunk, 0) + outer] = total.astype(recv.dtype)

    flying = [[] for _ in range(stages)]
    for chunk in range(chunks + 1):
        if chunk < chunks:
            produce(chunk, columns(chunk))
            flying[0].append(start(0, chunk))
        if chunk > 0:
            wait_landed(flying[0][chunk - 1])
            add(0, chunk - 1)
            flying[1].append(start(1, chunk - 1))
    for tick in range(chunks + 2 * (stages - 2)):
        for stage in range(1, stages):
            chunk = tick - 2 * (stage - 1)
            if 0 <= chunk < chunks:
                wait_landed(flying[stage][chunk])
                add(stage, chunk)
                if stage + 1 < stages:
                    flying[stage + 1].append(start(stage + 1, chunk))
    return [copy for groups in flying for group in groups for copy in group]


def gather_parts(place, chunks, out_ref, use, sems):
    stages = len(place.digits)
    width = out_ref.shape[-1] // chunks

    def columns(chunk):
        return slice(None) if chunks == 1 else pl.ds(chunk * width, width)

    def start(stage, chunk):
        index = (slice(None),) * (stages - 1 - stage) + place.block()[stages - 1 - stage :]
        held = out_ref.at[index + (slice(None), columns(chunk))]
        return [
            send(
                held,
                held,
                sems[2 * stage].at[chunk, step - 1],
                sems[2 * stage + 1].at[chunk, step - 1],
                place.device(stage, step),
            )
            for step in range(1, place.digits[stage])
        ]

    flying = [[] for _ in range(stages)]
    flying[stages - 1] = [start(stages - 1, chunk) for chunk in range(chunks)]
    for tick in range(chunks + stages + 1):
        for spot in range(stages):
            stage = stages - 2 - spot
            chunk = tick - spot - (1 if stage == 0 else 2 if stage < 0 else 0)
            if 0 <= chunk < chunks:
                wait_landed(flying[stage + 1][chunk])
                if stage < 0:
                    use(chunk, columns(chunk))
                else:
                    flying[stage].append(start(stage, chunk))
    return [copy for groups in flying for group in groups for copy in group]


def sem_shapes(digits, chunks):
    shapes = []
    for radix in digits:
        shapes += [pltpu.SemaphoreType.DMA((chunks, radix - 1))] * 2
    return shapes


def recv_shapes(digits, chunks, rows, width):
    return [
        pltpu.VMEM(
            (chunks, radix - 1) + tuple(reversed(digits[stage + 1 :])) + (rows, width), jnp.bfloat16
        )
        for stage, radix in enumerate(digits)
    ]


def params(number, mebibytes):
    return pltpu.CompilerParams(
        collective_id=number, has_side_effects=True, vmem_limit_bytes=mebibytes * 1024 * 1024
    )


def nothing(chunk, columns):
    return None


VMEM = pl.BlockSpec(memory_space=pltpu.VMEM)


def all_sum(x, devices, number):
    digits = radices(devices, 4)
    count = len(digits)
    shape = tuple(reversed(digits))
    rows, width = x.shape[0] // devices, x.shape[1]

    def kernel(x_ref, out_ref, *scratch):
        recvs, sems = scratch[:count], scratch[count:]
        place = Place(digits)
        place.barrier()

        def finish(chunk, columns, total):
            out_ref[place.block()] = total.astype(out_ref.dtype)

        copies = reduce_parts(place, 1, x_ref, nothing, finish, recvs, sems[: 2 * count])
        copies += gather_parts(place, 1, out_ref, nothing, sems[2 * count :])
        for copy in copies:
            copy.wait_send()

    out = pl.pallas_call(
        kernel,
        out_shape=jax.ShapeDtypeStruct(shape + (rows, width), jnp.bfloat16),
        in_specs=[VMEM],
        out_specs=VMEM,
        scratch_shapes=recv_shapes(digits, 1, rows, width) + sem_shapes(digits, 1) * 2,
        compiler_params=params(number, 8),
        name="all_sum",
    )(x.reshape(shape + (rows, width)))
    return out.reshape(x.shape)


def project_scatter(piece, weight, devices, chunks, number):
    digits = radices(devices, 2)
    count = len(digits)
    shape = tuple(reversed(digits))
    rows, width = piece.shape[0] // devices, weight.shape[1]

    def kernel(piece_ref, weight_ref, out_ref, x_ref, *scratch):
        recvs, sems = scratch[:count], scratch[count:]
        place = Place(digits)
        place.barrier()

        def produce(chunk, columns):
            part = jnp.dot(
                piece_ref[...], weight_ref[:, columns], preferred_element_type=jnp.float32
            ).astype(jnp.bfloat16)
            x_ref[(slice(None),) * (count + 1) + (columns,)] = part.reshape(
                shape + (rows, width // chunks)
            )

        def finish(chunk, columns, total):
            out_ref[:, columns] = total

        copies = reduce_parts(place, chunks, x_ref, produce, finish, recvs, sems)
        for copy in copies:
            copy.wait_send()

    return pl.pallas_call(
        kernel,
        out_shape=jax.ShapeDtypeStruct((rows, width), jnp.float32),
        in_specs=[VMEM, VMEM],
        out_specs=VMEM,
        scratch_shapes=[pltpu.VMEM(shape + (rows, width), jnp.bfloat16)]
        + recv_shapes(digits, chunks, rows, width // chunks)
        + sem_shapes(digits, chunks),
        compiler_params=params(number, 40),
        name="project_scatter",
    )(piece, weight)


def run_expert(packed, w_gate, w_up, w_down, devices, chunks, number):
    digits = radices(devices, 2)
    count = len(digits)
    shape = tuple(reversed(digits))
    rows, width = packed.shape
    units = w_gate.shape[1]
    tokens = devices * rows

    def kernel(
        packed_ref, gate_ref, up_ref, down_ref, out_ref,
        all_ref, x_ref, both_ref, lower_ref, sum_ref, hidden_ref, load_sems, *scratch
    ):
        recvs, sems = scratch[:count], scratch[count:]
        loads = [
            pltpu.make_async_copy(gate_ref, both_ref.at[:, pl.ds(0, units)], load_sems.at[0]),
            pltpu.make_async_copy(up_ref, both_ref.at[:, pl.ds(units, units)], load_sems.at[1]),
            pltpu.make_async_copy(down_ref, lower_ref, load_sems.at[2]),
        ]
        for load in loads:
            load.start()
        place = Place(digits)
        all_ref[place.block()] = packed_ref[...]
        place.barrier()

        def use(chunk, columns):
            if chunk == 0:
                loads[0].wait()
                loads[1].wait()
            part = jnp.dot(
                all_ref[(slice(None),) * (count + 1) + (columns,)].reshape(tokens, width // chunks),
                both_ref[columns, :],
                preferred_element_type=jnp.float32,
            )
            if chunk == 0:
                sum_ref[...] = part
            else:
                sum_ref[...] += part

        copies = gather_parts(place, chunks, all_ref, use, sems[: 2 * count])
        hidden_ref[...] = (jax.nn.silu(sum_ref[:, :units]) * sum_ref[:, units:]).astype(jnp.bfloat16)
        loads[2].wait()

        def produce(chunk, columns):
            part = jnp.dot(
                hidden_ref[...], lower_ref[:, columns], preferred_element_type=jnp.float32
            ).astype(jnp.bfloat16)
            x_ref[(slice(None),) * (count + 1) + (columns,)] = part.reshape(
                shape + (rows, width // chunks)
            )

        def finish(chunk, columns, total):
            out_ref[:, columns] = total

        copies += reduce_parts(
            place, chunks, x_ref, produce, finish, recvs, sems[2 * count :]
        )
        for copy in copies:
            copy.wait_send()

    return pl.pallas_call(
        kernel,
        out_shape=jax.ShapeDtypeStruct((rows, width), jnp.float32),
        in_specs=[VMEM] + [pl.BlockSpec(memory_space=pl.ANY)] * 3,
        out_specs=VMEM,
        scratch_shapes=[
            pltpu.VMEM(shape + (rows, width), jnp.bfloat16),
            pltpu.VMEM(shape + (rows, width), jnp.bfloat16),
            pltpu.VMEM((width, 2 * units), jnp.bfloat16),
            pltpu.VMEM((units, width), jnp.bfloat16),
            pltpu.VMEM((tokens, 2 * units), jnp.float32),
            pltpu.VMEM((tokens, units), jnp.bfloat16),
            pltpu.SemaphoreType.DMA((3,)),
        ]
        + recv_shapes(digits, chunks, rows, width // chunks)
        + sem_shapes(digits, chunks) * 2,
        compiler_params=params(number, 56),
        name="run_expert",
    )(packed, w_gate, w_up, w_down)


def convolve(mixer_in, conv_tail, conv_weight, conv_bias):
    width = mixer_in.shape[1]
    inputs = mixer_in.reshape(STEPS, REQ, width).astype(jnp.float32)
    history = jnp.concatenate([conv_tail.astype(jnp.float32), inputs], axis=0)
    kernel = conv_weight.astype(jnp.float32)
    summed = conv_bias[None, None, :] + kernel[0] * history[0:STEPS]
    for offset in range(1, CONV):
        summed = summed + kernel[offset] * history[offset : offset + STEPS]
    return jax.nn.silu(summed).astype(jnp.bfloat16).reshape(STEPS * REQ, width)


def run_states(mixed, gate_in, delta, b_part, c_part, ssm_state, decay_log, skip_gain):
    rate = -jnp.exp(decay_log)
    state = ssm_state.astype(jnp.float32)
    results = []
    for position in range(STEPS):
        first = position * REQ
        step_delta = delta[first : first + REQ]
        step_input = mixed[first : first + REQ].astype(jnp.float32)
        decay = jnp.exp(step_delta[:, None, :] * rate[None, :, :])
        state = (
            decay * state
            + (step_delta * step_input)[:, None, :] * b_part[first : first + REQ][:, :, None]
        )
        reading = (
            jnp.sum(c_part[first : first + REQ][:, :, None] * state, axis=1)
            + skip_gain[None, :] * step_input
        )
        results.append(reading * jax.nn.silu(gate_in[first : first + REQ].astype(jnp.float32)))
    return (jnp.concatenate(results, axis=0).astype(jnp.bfloat16), state.astype(jnp.bfloat16))


def route_inputs(hidden_state, expert_ids, norm_gain, router_weight):
    scale = lax.rsqrt(jnp.mean(hidden_state * hidden_state, axis=1, keepdims=True) + EPSILON)
    normed = (hidden_state * scale * norm_gain.astype(jnp.float32)[None, :]).astype(jnp.bfloat16)
    logits = jnp.dot(normed, router_weight, preferred_element_type=jnp.float32)
    labels = jnp.arange(logits.shape[1], dtype=jnp.int32)
    onehot = expert_ids[:, :, None] == labels[None, None, :]
    picked = jnp.sum(jnp.where(onehot, logits[:, None, :], 0.0), axis=2)
    weight_first = jax.nn.sigmoid(picked[:, 0] - picked[:, 1])
    weight_second = jax.nn.sigmoid(picked[:, 1] - picked[:, 0])
    route_weight = jnp.where(
        expert_ids[:, 0] == 0, weight_first, jnp.where(expert_ids[:, 1] == 0, weight_second, 0.0)
    )
    return (normed, route_weight)


def slot_matrix(own_ids, route_weight, most):
    member = jnp.logical_or(own_ids[:, 0] == 0, own_ids[:, 1] == 0).astype(jnp.int32)
    ranked = jnp.cumsum(member, dtype=jnp.int32) - member
    slots = jnp.arange(most, dtype=jnp.int32)
    choose = jnp.logical_and(member[None, :] > 0, ranked[None, :] == slots[:, None])
    choose_real = choose.astype(jnp.float32)
    return (choose_real, choose_real * route_weight[None, :])


def per_device(
    mixer_in,
    gate_in,
    conv_tail,
    ssm_state,
    resid,
    expert_ids,
    conv_weight,
    conv_bias,
    x_weight,
    dt_weight,
    dt_bias,
    decay_log,
    skip_gain,
    out_weight,
    norm_gain,
    router_weight,
    w_gate,
    w_up,
    w_down,
):
    devices = lax.axis_size("tensor")
    tokens_total = mixer_in.shape[0]
    own_count = tokens_total // devices
    most = max(2, own_count * TOPK * 3 // EXPERTS)
    most = (most + 15) // 16 * 16
    mixed = convolve(mixer_in, conv_tail, conv_weight, conv_bias)
    partial_proj = jnp.dot(mixed, x_weight, preferred_element_type=jnp.float32)
    projected = all_sum(partial_proj.astype(jnp.bfloat16), devices, 0).astype(jnp.float32)
    rank_part = projected[:, :RANK].astype(jnp.bfloat16)
    delta = jax.nn.softplus(
        jnp.dot(rank_part, dt_weight, preferred_element_type=jnp.float32) + dt_bias[None, :]
    )
    b_part = projected[:, RANK : RANK + STATE]
    c_part = projected[:, RANK + STATE :]
    readout, state_out = run_states(
        mixed, gate_in, delta, b_part, c_part, ssm_state, decay_log, skip_gain
    )
    position = lax.axis_index("tensor")
    mixer_rows = project_scatter(readout, out_weight, devices, 16, 1)
    own_ids = lax.dynamic_slice_in_dim(expert_ids, position * own_count, own_count, 0)
    hidden_state = resid.astype(jnp.float32) + mixer_rows
    normed, route_weight = route_inputs(hidden_state, own_ids, norm_gain, router_weight)
    choose_real, coefficient = slot_matrix(own_ids, route_weight, most)
    packed = jnp.dot(
        choose_real.astype(jnp.bfloat16), normed, preferred_element_type=jnp.float32
    ).astype(jnp.bfloat16)
    summed = run_expert(packed, w_gate, w_up, w_down, devices, 8, 2)
    expert_rows = jnp.dot(coefficient.T, summed, precision=lax.Precision.HIGHEST)
    layer_out = (hidden_state + expert_rows).astype(jnp.bfloat16)
    return (layer_out, state_out)


def solution(mesh):
    return jax.shard_map(
        per_device,
        mesh=mesh,
        in_specs=(
            P("groups", "tensor"),
            P("groups", "tensor"),
            P(None, "groups", "tensor"),
            P("groups", None, "tensor"),
            P(("groups", "tensor"), None),
            P("groups", None),
            P(None, "tensor"),
            P("tensor"),
            P("tensor", None),
            P(None, "tensor"),
            P("tensor"),
            P(None, "tensor"),
            P("tensor"),
            P("tensor", None),
            P(),
            P(),
            P(None, "tensor"),
            P(None, "tensor"),
            P("tensor", None),
        ),
        out_specs=(P(("groups", "tensor"), None), P("groups", None, "tensor")),
        check_vma=False,
    )
```
